32 devices in a mesh: seq: 16 (over z, x, core), mem: 2 (over y).
Axes of the slice: x: 2, y: 2, z: 4, core: 2. Of those that a mesh axis runs over, the one named last changes fastest.
Arguments:
- inputs: bfloat16 [4096, 1024], P('seq'), may hold values from -6 to 6
- memory: bfloat16 [64, 128, 1024], P('seq', 'mem'), may hold values from -6 to 6
- cotangent: bfloat16 [4096, 1024], P('seq'), may hold values from -6 to 6
- is_long: int32 [16], P('seq'), may hold values from 0 to 1, as said below
- memory_len: int32 [64], P('seq'), may hold values from 0 to 128, as said below
- distance_bucket: int32 [256], replicated, may hold values from 0 to 31, as said below
- norm_self: float32 [1024], replicated, may hold values from 0.5 to 1.5
- query_self: bfloat16 [1024, 1024], replicated, may hold values from -0.046875 to 0.046875
- key_self: bfloat16 [1024, 512], replicated, may hold values from -0.1875 to 0.1875
- value_self: bfloat16 [1024, 512], replicated, may hold values from -0.1875 to 0.1875
- output_self: bfloat16 [1024, 1024], replicated, may hold values from -0.5 to 0.5
- bias_table: float32 [32, 16], replicated, may hold values from -4 to 4
- norm_cross: float32 [1024], replicated, may hold values from 0.5 to 1.5
- query_cross: bfloat16 [1024, 1024], replicated, may hold values from -0.046875 to 0.046875
- key_cross: bfloat16 [1024, 512], replicated, may hold values from -0.1875 to 0.1875
- value_cross: bfloat16 [1024, 512], replicated, may hold values from -0.1875 to 0.1875
- output_cross: bfloat16 [1024, 1024], replicated, may hold values from -0.5 to 0.5
- norm_feed: float32 [1024], replicated, may hold values from 0.5 to 1.5
- gate_proj: bfloat16 [1024, 2816], replicated, may hold values from -0.1875 to 0.1875
- up_proj: bfloat16 [1024, 2816], replicated, may hold values from -0.1875 to 0.1875
- down_proj: bfloat16 [2816, 1024], replicated, may hold values from -0.109375 to 0.109375
Outputs:
- outputs: bfloat16 [4096, 1024], P('seq')
- inputs_grad: float32 [4096, 1024], P('seq')
- memory_grad: float32 [64, 128, 1024], P('seq', 'mem')
- norm_self_grad: float32 [1024], P('seq')
- query_self_grad: float32 [1024, 1024], P('seq')
- key_self_grad: float32 [1024, 512], P('seq')
- value_self_grad: float32 [1024, 512], P('seq')
- output_self_grad: float32 [1024, 1024], P('seq')
- bias_table_grad: float32 [32, 16], replicated
- norm_cross_grad: float32 [1024], P('seq')
- query_cross_grad: float32 [1024, 1024], P('seq')
- key_cross_grad: float32 [1024, 512], P(('seq', 'mem'))
- value_cross_grad: float32 [1024, 512], P(('seq', 'mem'))
- output_cross_grad: float32 [1024, 1024], P('seq')
- norm_feed_grad: float32 [1024], P('seq')
- gate_proj_grad: float32 [1024, 2816], P('seq')
- up_proj_grad: float32 [1024, 2816], P('seq')
- down_proj_grad: float32 [2816, 1024], P('seq')
The draws below stay inside these ranges and needn't reach their ends.
Inputs may be any that keep to these rules, and one draw needn't show every extreme that they name: `is_long`: exactly 5 entries are 1, the others 0. `memory_len`: entry 4 * i + s belongs to slot s of group i. Where is_long[i] is 1, slot 0 holds more than 64 positions and the other slots 0; elsewhere every slot holds more than 64. Some slot 0 holds exactly 128. `distance_bucket`: entry d is the bucket of distance d: d itself below 16, never falling, rising by at most one from one distance to the next, and 31 at distance 256 - 1.
All inputs are finite; a program needn't handle non-finite values.
Results may differ from the reference program's by a relative error of at most 0.02.
The reference program's roundings to bfloat16 on the way count: a program that leaves them out, or rounds other values in their place, can miss the bound.
Values may be sent and summed in bfloat16 or wider, within the bound.
A program may use at most 256 MiB of HBM per device.

```python
import jax
import jax.numpy as jnp
from jax import lax

D = 1024
HEADS = 16
KV_HEADS = 8
HEAD_DIM = 64
FF = 2816
BUCKETS = 32
SHORT = 64
SLOTS = 4
MEMW = 128
TGT = 256
TOKENS = 4096
MSLOTS = 64
N_LONG = 5
N_SEQ = 16


def long_flags(key):
    order = jax.random.permutation(key, N_SEQ)
    return (order < N_LONG).astype(jnp.int32)


def draw_is_long(key, part):
    return long_flags(key)


def draw_memory_len(key, part):
    flags = long_flags(key)
    key = jax.random.fold_in(key, 7)
    first_key, second_key = jax.random.split(key)
    half_width = MEMW // 2
    lengths = jax.random.randint(first_key, (N_SEQ, SLOTS), half_width + 1, MEMW + 1)
    slot_index = jnp.arange(SLOTS)[None, :]
    lengths = jnp.where((flags[:, None] == 1) & (slot_index > 0), 0, lengths)
    picked = jax.random.randint(second_key, (), 0, N_SEQ)
    lengths = jnp.where((jnp.arange(N_SEQ)[:, None] == picked) & (slot_index == 0), MEMW, lengths)
    return lengths.reshape(-1).astype(jnp.int32)


def draw_distance_bucket(key, part):
    key = jax.random.fold_in(key, 11)
    bounds = jax.random.choice(key, jnp.arange(17, TGT), (BUCKETS - 17,), replace=False)
    distance = jnp.arange(TGT)
    farther = 16 + jnp.sum((bounds[None, :] <= distance[:, None]).astype(jnp.int32), axis=1)
    return jnp.where(distance < 16, distance, farther).astype(jnp.int32)


def steps_of(key, extent, pieces, low, top_value):
    def one(dim, blocks):
        draws = jax.random.uniform(jax.random.fold_in(jax.random.fold_in(key, 6), dim), (blocks,), jnp.float32, low / len(pieces), top_value / len(pieces))
        return jnp.repeat(jnp.exp(draws), extent[dim] // blocks).reshape((-1,) + (1,) * (len(extent) - dim - 1))

    loudness = one(*pieces[0])
    for cut in pieces[1:]:
        loudness = loudness * one(*cut)
    return loudness


def normal_values(own_key, shape, spread, bound, shards=(), dtype=jnp.bfloat16):
    factor_of = steps_of(own_key, shape, shards, -0.22, 0.18) if shards else 1.0
    values = jax.random.normal(own_key, shape, jnp.float32) * spread * factor_of
    return jnp.minimum(jnp.maximum(values, -bound), bound).astype(dtype)


def setup_inputs(seed: int = 0) -> dict:
    key_of = jax.random.split(jax.random.key(seed), 22)
    inputs = normal_values(key_of[0], (TOKENS, D), 1.0, 6.0, ((0, 16),))
    memory = normal_values(key_of[1], (MSLOTS, MEMW, D), 1.0, 6.0, ((0, 16), (1, 2)))
    cotangent = normal_values(key_of[2], (TOKENS, D), 1.0, 6.0, ((0, 16),))
    is_long = draw_is_long(jax.random.fold_in(key_of[21], 71), 0)
    memory_len = draw_memory_len(jax.random.fold_in(key_of[21], 71), 0)
    distance_bucket = draw_distance_bucket(jax.random.fold_in(key_of[21], 71), 0)
    norm_self = jnp.clip(1.0 + 0.1 * jax.random.normal(key_of[6], (D,), jnp.float32), 0.5, 1.5)
    query_self = normal_values(key_of[7], (D, D), (16 * D) ** -0.5, 0.046875)
    key_self = normal_values(key_of[8], (D, KV_HEADS * HEAD_DIM), D ** -0.5, 0.1875)
    value_self = normal_values(key_of[9], (D, KV_HEADS * HEAD_DIM), D ** -0.5, 0.1875)
    output_self = normal_values(key_of[10], (D, D), (D // 8) ** -0.5, 0.5)
    bias_table = normal_values(key_of[11], (BUCKETS, HEADS), 1.0, 4.0, (), jnp.float32)
    norm_cross = jnp.clip(1.0 + 0.1 * jax.random.normal(key_of[12], (D,), jnp.float32), 0.5, 1.5)
    query_cross = normal_values(key_of[13], (D, D), (16 * D) ** -0.5, 0.046875)
    key_cross = normal_values(key_of[14], (D, KV_HEADS * HEAD_DIM), D ** -0.5, 0.1875)
    value_cross = normal_values(key_of[15], (D, KV_HEADS * HEAD_DIM), D ** -0.5, 0.1875)
    output_cross = normal_values(key_of[16], (D, D), (D // 8) ** -0.5, 0.5)
    norm_feed = jnp.clip(1.0 + 0.1 * jax.random.normal(key_of[17], (D,), jnp.float32), 0.5, 1.5)
    gate_proj = normal_values(key_of[18], (D, FF), D ** -0.5, 0.1875)
    up_proj = normal_values(key_of[19], (D, FF), D ** -0.5, 0.1875)
    down_proj = normal_values(key_of[20], (FF, D), FF ** -0.5, 0.109375)
    return dict(inputs=inputs, memory=memory, cotangent=cotangent, is_long=is_long, memory_len=memory_len, distance_bucket=distance_bucket, norm_self=norm_self, query_self=query_self, key_self=key_self, value_self=value_self, output_self=output_self, bias_table=bias_table, norm_cross=norm_cross, query_cross=query_cross, key_cross=key_cross, value_cross=value_cross, output_cross=output_cross, norm_feed=norm_feed, gate_proj=gate_proj, up_proj=up_proj, down_proj=down_proj)


@jax.custom_vjp
def low(v):
    return lax.optimization_barrier(v.astype(jnp.bfloat16)).astype(jnp.float32)

@jax.custom_vjp
def low_back(v):
    return v

def low_keep(v):
    return (low(v), None)

def low_pass(kept, grad):
    return (grad,)

def back_keep(v):
    return (v, None)

def back_low(kept, grad):
    return (low(grad),)
low.defvjp(low_keep, low_pass)
low_back.defvjp(back_keep, back_low)
HIGHEST = lax.Precision.HIGHEST

def product(left_side, right_side):
    return jnp.dot(left_side, right_side, precision=HIGHEST)

def rms_norm(values, gain):
    return values * lax.rsqrt(lax.optimization_barrier(jnp.mean(values * values, axis=-1, keepdims=True)) + 1e-06) * gain

def round_both(values):
    return low(low_back(values))

def masked_softmax(scores, allowed):
    return jax.nn.softmax(jnp.where(allowed, scores, -1e+30), axis=-1)

def decoder_layer(inputs, memory, long_flag, lengths, distance_bucket, norm_self, query_self, key_self, value_self, output_self, bias_table, norm_cross, query_cross, key_cross, value_cross, output_cross, norm_feed, gate_proj, up_proj, down_proj):
    targets = inputs.shape[0]
    group_size = HEADS // KV_HEADS
    positions = jnp.arange(targets)
    hidden_one = low(rms_norm(inputs, norm_self))
    queries = round_both(product(hidden_one, query_self)).reshape(targets, KV_HEADS, group_size, HEAD_DIM)
    keys_self = round_both(product(hidden_one, key_self)).reshape(targets, KV_HEADS, HEAD_DIM)
    values_self = round_both(product(hidden_one, value_self)).reshape(targets, KV_HEADS, HEAD_DIM)
    distance = positions[:, None] - positions[None, :]
    bias_full = bias_table[distance_bucket[jnp.clip(distance, 0, targets - 1)]]
    bias_full = jnp.transpose(bias_full, (2, 0, 1)).reshape(KV_HEADS, group_size, targets, targets)
    scores = jnp.einsum('tkrd,ukd->krtu', queries, keys_self, precision=HIGHEST) + bias_full
    scores = low_back(scores)
    seq_span = jnp.where(long_flag == 1, targets, SHORT)
    allowed = (distance >= 0) & (positions[:, None] // seq_span == positions[None, :] // seq_span)
    attention = low(masked_softmax(scores, allowed))
    attended = jnp.einsum('krtu,ukd->tkrd', attention, values_self, precision=HIGHEST).reshape(targets, D)
    after_self = inputs + low_back(product(round_both(attended), output_self))
    hidden_two = low(rms_norm(after_self, norm_cross))
    cross_queries = round_both(product(hidden_two, query_cross)).reshape(SLOTS, SHORT, KV_HEADS, group_size, HEAD_DIM)
    memory_rows = memory.reshape(-1, D)
    memory_keys = round_both(product(memory_rows, key_cross)).reshape(SLOTS, MEMW, KV_HEADS, HEAD_DIM)
    memory_values = round_both(product(memory_rows, value_cross)).reshape(SLOTS, MEMW, KV_HEADS, HEAD_DIM)
    chosen = jnp.where(long_flag == 1, 0, jnp.arange(SLOTS))
    chosen_keys = memory_keys[chosen]
    chosen_values = memory_values[chosen]
    chosen_lengths = lengths[chosen]
    cross_scores = low_back(jnp.einsum('bskrd,bmkd->bkrsm', cross_queries, chosen_keys, precision=HIGHEST))
    valid = jnp.arange(MEMW)[None, :] < chosen_lengths[:, None]
    cross_attention = low(masked_softmax(cross_scores, valid[:, None, None, None, :]))
    cross_attended = jnp.einsum('bkrsm,bmkd->bskrd', cross_attention, chosen_values, precision=HIGHEST).reshape(targets, D)
    after_cross = after_self + low_back(product(round_both(cross_attended), output_cross))
    hidden_three = low(rms_norm(after_cross, norm_feed))
    gate_values = low_back(product(hidden_three, gate_proj))
    up_values = low_back(product(hidden_three, up_proj))
    activated = low(jax.nn.gelu(gate_values, approximate=True) * up_values)
    return after_cross + low_back(product(activated, down_proj))

def reference(inputs, memory, cotangent, is_long, memory_len, distance_bucket, norm_self, query_self, key_self, value_self, output_self, bias_table, norm_cross, query_cross, key_cross, value_cross, output_cross, norm_feed, gate_proj, up_proj, down_proj):
    weights = tuple((item.astype(jnp.float32) for item in (norm_self, query_self, key_self, value_self, output_self, bias_table, norm_cross, query_cross, key_cross, value_cross, output_cross, norm_feed, gate_proj, up_proj, down_proj)))
    inputs_all = inputs.astype(jnp.float32).reshape(N_SEQ, TGT, D)
    memory_all = memory.astype(jnp.float32).reshape(N_SEQ, SLOTS, MEMW, D)
    upstream_all = cotangent.astype(jnp.float32).reshape(N_SEQ, TGT, D)
    lengths_all = memory_len.reshape(N_SEQ, SLOTS)

    def one_unit(totals, item):
        inputs_one, memory_one, upstream_one, long_flag, lengths_one = item

        def forward(inputs_value, memory_value, *params):
            return decoder_layer(inputs_value, memory_value, long_flag, lengths_one, distance_bucket, *params)
        result, backward = jax.vjp(forward, inputs_one, memory_one, *weights)
        gradients = backward(upstream_one)
        totals = tuple((total + part for total, part in zip(totals, gradients[2:])))
        return (totals, (result, gradients[0], gradients[1]))
    zeros = tuple((jnp.zeros_like(item) for item in weights))
    totals, (results, inputs_grads, memory_grads) = lax.scan(one_unit, zeros, (inputs_all, memory_all, upstream_all, is_long, lengths_all))
    return (results.reshape(N_SEQ * TGT, D).astype(jnp.bfloat16), inputs_grads.reshape(N_SEQ * TGT, D), memory_grads.reshape(N_SEQ * SLOTS, MEMW, D), totals[0], totals[1], totals[2], totals[3], totals[4], totals[5], totals[6], totals[7], totals[8], totals[9], totals[10], totals[11], totals[12], totals[13], totals[14])
```

```python
import functools

import jax
import jax.numpy as jnp
from jax import lax
from jax.experimental import pallas as pl
from jax.experimental.pallas import tpu as pltpu
from jax.sharding import PartitionSpec as P

HEAD_DIM = 64
BUCKETS = 32
SHORT = 64
SLOTS = 4
EPSILON = 1e-06
MASKED = -1e30
TILE = 256
VMEM_LIMIT = 60 * 2**20
F32 = jnp.float32
BF16 = jnp.bfloat16
GELU_C = 0.7978845608028654
GELU_A = 0.044715


def dot_nn(left, right):
    return lax.dot_general(left, right, (((1,), (0,)), ((), ())), preferred_element_type=F32)


def dot_nt(left, right):
    return lax.dot_general(left, right, (((1,), (1,)), ((), ())), preferred_element_type=F32)


def dot_tn(left, right):
    return lax.dot_general(left, right, (((0,), (0,)), ((), ())), preferred_element_type=F32)


def scaling_of(values):
    return lax.rsqrt(jnp.mean(values * values, axis=-1, keepdims=True) + EPSILON)


def norm_back(values, gain, upstream):
    scaling = scaling_of(values)
    normed = values * scaling
    scaled = upstream * gain
    through = scaling * (scaled - normed * jnp.mean(scaled * normed, axis=-1, keepdims=True))
    return through, jnp.sum(upstream * normed, axis=0, keepdims=True)


def tiles(count, body):
    @pl.loop(0, count)
    def _(j):
        body(pl.ds(pl.multiple_of(j * TILE, TILE), TILE))


def start_all(sources, targets, sems):
    copies = [
        pltpu.make_async_copy(source, target, sems.at[i])
        for i, (source, target) in enumerate(zip(sources, targets, strict=True))
    ]
    for copy in copies:
        copy.start()
    return copies


def two_rows(pair):
    return jnp.concatenate([pair[:, :HEAD_DIM], pair[:, HEAD_DIM:]], axis=0)


def two_columns(stack):
    rows = stack.shape[0] // 2
    return jnp.concatenate([stack[:rows], stack[rows:]], axis=1)


def self_forward(
    long_ref, x_ref, gain_ref, bias_ref, wq_hbm, wk_hbm, wv_hbm, wo_hbm,
    h_ref, q_ref, k_ref, v_ref, att_ref, p_ref, out_ref,
    wq, wk, wv, wo, sems,
):
    copies = start_all((wq_hbm, wk_hbm, wv_hbm, wo_hbm), (wq, wk, wv, wo), sems)
    rows, width = x_ref.shape
    is_long = long_ref[0] == 1
    x = x_ref[...].astype(F32)
    h_ref[...] = (x * scaling_of(x) * gain_ref[...]).astype(BF16)
    for copy, weight, result in zip(copies, (wq, wk, wv), (q_ref, k_ref, v_ref)):
        copy.wait()

        def project(columns, weight=weight, result=result):
            result[:, columns] = dot_nn(h_ref[...], weight[:, columns]).astype(BF16)

        tiles(weight.shape[1] // TILE, project)

    t = lax.broadcasted_iota(jnp.int32, (rows, rows), 0)
    u = lax.broadcasted_iota(jnp.int32, (rows, rows), 1)
    allowed = (u <= t) & (is_long | (t // SHORT == u // SHORT))

    @pl.loop(0, k_ref.shape[1] // 128)
    def _(pair):
        k_pair = k_ref[:, pl.ds(pl.multiple_of(pair * 128, 128), 128)]
        v_pair = v_ref[:, pl.ds(pl.multiple_of(pair * 128, 128), 128)]
        for i in range(2):
            lanes = slice(i * HEAD_DIM, (i + 1) * HEAD_DIM)
            columns = pl.ds(pl.multiple_of(pair * 256 + i * 128, 128), 128)
            q_pair = q_ref[:, columns]
            parts = []
            for h in range(2):
                head = pair * 4 + i * 2 + h
                scores = dot_nt(q_pair[:, h * HEAD_DIM : (h + 1) * HEAD_DIM], k_pair[:, lanes])
                bias = jnp.broadcast_to(bias_ref[pl.ds(head, 1), :], (rows, rows))
                scores += pltpu.roll(bias, 0, 1, stride=1, stride_axis=0)
                scores = jnp.where(allowed, scores, MASKED)
                weights = jnp.exp(scores - jnp.max(scores, axis=-1, keepdims=True))
                weights = weights / jnp.sum(weights, axis=-1, keepdims=True)
                p_ref[pair * 2 + i, h * rows : (h + 1) * rows, :] = weights
                parts.append(dot_nn(weights.astype(BF16), v_pair[:, lanes]))
            att_ref[:, columns] = jnp.concatenate(parts, axis=1).astype(BF16)

    copies[3].wait()

    def leave(columns):
        out_ref[:, columns] = x_ref[:, columns].astype(F32) + dot_nn(att_ref[...], wo[:, columns])

    tiles(width // TILE, leave)


def cross_and_feed(
    long_ref, len_ref, x_ref, cot_ref, own_ref, other_ref, gain_ref, feed_gain_ref,
    wq_hbm, wo_hbm, gate_hbm, up_hbm, down_hbm,
    out_ref, grad_ref, feed_gain_grad_ref, h_ref, q_ref, att_ref, p_ref, chosen_ref,
    feed_ref, act_ref, gate_grad_ref, up_grad_ref,
    wq, wo, gate, up, down, acc, three, sems, feed_sems,
):
    copies = start_all((wq_hbm, wo_hbm), (wq, wo), sems)
    rows, width = x_ref.shape
    hidden = gate.shape[1]

    def feed_copies(j):
        columns = pl.ds(pl.multiple_of(j * TILE, TILE), TILE)
        return (
            pltpu.make_async_copy(gate_hbm.at[:, columns], gate.at[:, columns], feed_sems.at[0, j]),
            pltpu.make_async_copy(up_hbm.at[:, columns], up.at[:, columns], feed_sems.at[1, j]),
            pltpu.make_async_copy(down_hbm.at[columns, :], down.at[columns, :], feed_sems.at[2, j]),
        )

    @pl.loop(0, hidden // TILE)
    def _(j):
        for copy in feed_copies(j):
            copy.start()

    is_long = long_ref[0] == 1
    x = x_ref[...]
    h_ref[...] = (x * scaling_of(x) * gain_ref[...]).astype(BF16)

    me = lax.axis_index("mem")
    span = own_ref.shape[1]
    for part, ref in ((me, own_ref), (1 - me, other_ref)):
        positions = pl.ds(pl.multiple_of(part * span, span), span)
        for b in range(SLOTS):
            chosen_ref[b, positions, :] = jnp.where(is_long, ref[0], ref[b])

    copies[0].wait()

    def project(columns):
        q_ref[:, columns] = dot_nn(h_ref[...], wq[:, columns]).astype(BF16)

    tiles(width // TILE, project)
    slot_width = chosen_ref.shape[1]
    half = chosen_ref.shape[2] // 2
    positions = lax.broadcasted_iota(jnp.int32, (2 * SHORT, slot_width), 1)

    @pl.loop(0, half // 128)
    def _(pair):
        for i in range(2):
            columns = pl.ds(pl.multiple_of(pair * 256 + i * 128, 128), 128)
            lanes = slice(i * HEAD_DIM, (i + 1) * HEAD_DIM)
            for b in range(SLOTS):
                block = slice(b * SHORT, (b + 1) * SHORT)
                keys = chosen_ref[b, :, pl.ds(pl.multiple_of(pair * 128, 128), 128)][:, lanes]
                values = chosen_ref[b, :, pl.ds(pl.multiple_of(half + pair * 128, 128), 128)][:, lanes]
                length = jnp.where(is_long, len_ref[0], len_ref[b])
                scores = dot_nt(two_rows(q_ref[block, columns]), keys)
                scores = jnp.where(positions < length, scores, MASKED)
                weights = jnp.exp(scores - jnp.max(scores, axis=-1, keepdims=True))
                weights = weights / jnp.sum(weights, axis=-1, keepdims=True)
                p_ref[pair * 2 + i, b] = weights
                att_ref[block, columns] = two_columns(dot_nn(weights.astype(BF16), values)).astype(BF16)

    copies[1].wait()

    def leave(columns):
        acc[:, columns] = x_ref[:, columns] + dot_nn(att_ref[...], wo[:, columns])

    tiles(width // TILE, leave)
    x = acc[...]
    feed_ref[...] = (x * scaling_of(x) * feed_gain_ref[...]).astype(BF16)
    grad_ref[...] = x
    three[...] = jnp.zeros_like(three)

    @pl.loop(0, hidden // TILE)
    def _(j):
        for copy in feed_copies(j):
            copy.wait()
        columns = pl.ds(pl.multiple_of(j * TILE, TILE), TILE)
        g = dot_nn(feed_ref[...], gate[:, columns])
        u = dot_nn(feed_ref[...], up[:, columns])
        square = g * g
        tanh = jnp.tanh(GELU_C * (g + GELU_A * g * square))
        gelu = 0.5 * g * (1.0 + tanh)
        act = (gelu * u).astype(BF16)
        act_ref[:, columns] = act
        acc[...] += dot_nn(act, down[columns, :])
        act_grad = dot_nt(cot_ref[...], down[columns, :])
        slope = 0.5 * (1.0 + tanh) + 0.5 * g * (1.0 - tanh * tanh) * (
            GELU_C * (1.0 + 3.0 * GELU_A * square)
        )
        gate_grad = (act_grad * u * slope).astype(BF16)
        up_grad = (act_grad * gelu).astype(BF16)
        gate_grad_ref[:, columns] = gate_grad
        up_grad_ref[:, columns] = up_grad
        three[...] += dot_nt(gate_grad, gate[:, columns]) + dot_nt(up_grad, up[:, columns])

    out_ref[...] = acc[...].astype(BF16)
    through, gain_grad = norm_back(grad_ref[...], feed_gain_ref[...], three[...])
    feed_gain_grad_ref[...] = gain_grad
    grad_ref[...] = cot_ref[...].astype(F32) + through


def diagonal_sums(scores):
    rows, width = scores.shape
    while rows > 8:
        rows //= 2
        scores = scores[:rows] + pltpu.roll(scores[rows:], width - rows, 1)
    t = lax.broadcasted_iota(jnp.int32, scores.shape, 0)
    for bit in (4, 2, 1):
        scores = jnp.where((t & bit) != 0, pltpu.roll(scores, width - bit, 1), scores)
    return jnp.sum(scores, axis=0, keepdims=True)


def attention_back(weights, values, keys, queries, out_grad):
    values_grad = dot_tn(weights.astype(BF16), out_grad)
    weights_grad = dot_nt(out_grad, values)
    inner = jnp.sum(weights * weights_grad, axis=-1, keepdims=True)
    scores_grad = (weights * (weights_grad - inner)).astype(BF16)
    queries_grad = dot_nn(scores_grad, keys)
    keys_grad = dot_tn(scores_grad, queries)
    return queries_grad, keys_grad, values_grad, scores_grad


def gradient_into(result, left_ref, right_ref, columns):
    @pl.loop(0, left_ref.shape[1] // TILE)
    def _(j):
        rows = pl.ds(pl.multiple_of(j * TILE, TILE), TILE)
        result[rows, :] = dot_tn(left_ref[:, rows], right_ref[:, columns]).astype(result.dtype)


def backward(
    long_ref, x_ref, mid_ref, grad_ref, cot_ref, gain_one_ref, gain_two_ref,
    h1_ref, q_ref, k_ref, v_ref, att_ref, p_ref,
    h2_ref, cq_ref, catt_ref, cp_ref, chosen_ref, memory_ref,
    h3_ref, act_ref, gate_grad_ref, up_grad_ref,
    wq_hbm, wk_hbm, wv_hbm, wo_hbm, wcq_hbm, wck_hbm, wcv_hbm, wco_hbm,
    in_grad_ref, mem_grad_ref, diagonal_ref, gain_grad_ref,
    g_q, g_k, g_v, g_o, g_cq, g_co, g_gate, g_up, g_down, g_ck, g_cv,
    wq, wk, wv, wo, wcq, wck, wcv, wco,
    branch, out_grad, q_grad, k_grad, v_grad, mem_k, mem_v, wide, after, sems,
):
    hbm = (wco_hbm, wcq_hbm, wck_hbm, wcv_hbm, wo_hbm, wq_hbm, wk_hbm, wv_hbm)
    copies = start_all(hbm, (wco, wcq, wck, wcv, wo, wq, wk, wv), sems)
    rows, width = x_ref.shape
    half_pair = k_ref.shape[1] // 2
    half = width // 2
    half_hidden = act_ref.shape[1] // 2
    me = lax.axis_index("mem")
    is_long = long_ref[0] == 1

    def mine(size):
        return pl.ds(pl.multiple_of(me * size, 128), size)

    gradient_into(g_gate, h3_ref, gate_grad_ref, mine(half_hidden))
    gradient_into(g_up, h3_ref, up_grad_ref, mine(half_hidden))
    gradient_into(g_down, act_ref, cot_ref, mine(half))

    branch[...] = grad_ref[...].astype(BF16)
    gradient_into(g_co, catt_ref, branch, mine(half))
    copies[0].wait()

    def out_of_cross(columns):
        out_grad[:, columns] = dot_nt(branch[...], wco[columns, :]).astype(BF16)

    tiles(width // TILE, out_of_cross)
    slot_width = chosen_ref.shape[1]
    pair_width = k_ref.shape[1]

    @pl.loop(0, pair_width // 128)
    def _(pair):
        keys_at = pl.ds(pl.multiple_of(pair * 128, 128), 128)
        values_at = pl.ds(pl.multiple_of(pair_width + pair * 128, 128), 128)
        for b in range(SLOTS):
            block = slice(b * SHORT, (b + 1) * SHORT)
            keys_parts, values_parts = [], []
            for i in range(2):
                columns = pl.ds(pl.multiple_of(pair * 256 + i * 128, 128), 128)
                lanes = slice(i * HEAD_DIM, (i + 1) * HEAD_DIM)
                queries_part, keys_part, values_part, _ = attention_back(
                    cp_ref[pair * 2 + i, b],
                    chosen_ref[b, :, values_at][:, lanes],
                    chosen_ref[b, :, keys_at][:, lanes],
                    two_rows(cq_ref[block, columns]),
                    two_rows(out_grad[block, columns]),
                )
                q_grad[block, columns] = two_columns(queries_part).astype(BF16)
                keys_parts.append(keys_part)
                values_parts.append(values_part)
            mem_k[b, :, keys_at] = jnp.concatenate(keys_parts, axis=1)
            mem_v[b, :, keys_at] = jnp.concatenate(values_parts, axis=1)

    span = slot_width // 2
    positions = pl.ds(pl.multiple_of(me * span, span), span)
    for stack, result in ((mem_k, k_grad), (mem_v, v_grad)):
        total = stack[0, positions, :]
        for b in range(1, SLOTS):
            own = stack[b, positions, :]
            total += jnp.where(is_long, own, 0.0)
            result[b * span : (b + 1) * span, :] = jnp.where(is_long, 0.0, own).astype(BF16)
        result[0:span, :] = total.astype(BF16)
    gradient_into(g_ck, memory_ref, k_grad, slice(None))
    gradient_into(g_cv, memory_ref, v_grad, slice(None))
    gradient_into(g_cq, h2_ref, q_grad, mine(half))
    copies[1].wait()
    copies[2].wait()
    copies[3].wait()

    def into_cross(columns):
        mem_grad_ref[:, columns] = dot_nt(k_grad[...], wck[columns, :]) + dot_nt(
            v_grad[...], wcv[columns, :]
        )
        wide[:, columns] = dot_nt(q_grad[...], wcq[columns, :])

    tiles(width // TILE, into_cross)
    through, gain_grad = norm_back(mid_ref[...], gain_two_ref[...], wide[...])
    gain_grad_ref[1:2, :] = gain_grad
    after[...] = grad_ref[...] + through

    branch[...] = after[...].astype(BF16)
    gradient_into(g_o, att_ref, branch, mine(half))
    copies[4].wait()

    def out_of_self(columns):
        out_grad[:, columns] = dot_nt(branch[...], wo[columns, :]).astype(BF16)

    tiles(width // TILE, out_of_self)

    @pl.loop(0, pair_width // 128)
    def _(pair):
        at = pl.ds(pl.multiple_of(pair * 128, 128), 128)
        k_pair = k_ref[:, at]
        v_pair = v_ref[:, at]
        keys_parts, values_parts = [], []
        for i in range(2):
            columns = pl.ds(pl.multiple_of(pair * 256 + i * 128, 128), 128)
            lanes = slice(i * HEAD_DIM, (i + 1) * HEAD_DIM)
            queries_part, keys_part, values_part, scores_grad = attention_back(
                p_ref[pair * 2 + i],
                v_pair[:, lanes],
                k_pair[:, lanes],
                two_rows(q_ref[:, columns]),
                two_rows(out_grad[:, columns]),
            )
            q_grad[:, columns] = two_columns(queries_part).astype(BF16)
            keys_parts.append(keys_part)
            values_parts.append(values_part)
            for h in range(2):
                diagonal_ref[pl.ds(pair * 4 + i * 2 + h, 1), :] = diagonal_sums(
                    scores_grad[h * rows : (h + 1) * rows].astype(F32)
                )
        k_grad[:, at] = jnp.concatenate(keys_parts, axis=1).astype(BF16)
        v_grad[:, at] = jnp.concatenate(values_parts, axis=1).astype(BF16)

    gradient_into(g_q, h1_ref, q_grad, mine(half))
    gradient_into(g_k, h1_ref, k_grad, mine(half_pair))
    gradient_into(g_v, h1_ref, v_grad, mine(half_pair))
    for copy in copies[5:]:
        copy.wait()

    def into_self(columns):
        wide[:, columns] = (
            dot_nt(q_grad[...], wq[columns, :])
            + dot_nt(k_grad[...], wk[columns, :])
            + dot_nt(v_grad[...], wv[columns, :])
        )

    tiles(width // TILE, into_self)
    through, gain_grad = norm_back(x_ref[...].astype(F32), gain_one_ref[...], wide[...])
    gain_grad_ref[0:1, :] = gain_grad
    in_grad_ref[...] = after[...] + through


SMEM = pl.BlockSpec(memory_space=pltpu.SMEM)
VMEM = pl.BlockSpec(memory_space=pltpu.VMEM)
ANY = pl.BlockSpec(memory_space=pl.ANY)


def shape_of(shape, dtype):
    return jax.ShapeDtypeStruct(shape, dtype)


def scratch_like(*arrays):
    return [pltpu.VMEM(array.shape, array.dtype) for array in arrays]


def call(kernel, in_specs, outs, scratch, **params):
    return pl.pallas_call(
        kernel,
        in_specs=in_specs,
        out_specs=[VMEM] * len(outs),
        out_shape=[shape_of(*out) for out in outs],
        scratch_shapes=scratch,
        compiler_params=pltpu.CompilerParams(vmem_limit_bytes=VMEM_LIMIT, **params),
    )


def shards(
    seq_size,
    inputs,
    memory,
    cotangent,
    is_long,
    memory_len,
    distance_bucket,
    norm_self,
    query_self,
    key_self,
    value_self,
    output_self,
    bias_table,
    norm_cross,
    query_cross,
    key_cross,
    value_cross,
    output_cross,
    norm_feed,
    gate_proj,
    up_proj,
    down_proj,
):
    rows, width = inputs.shape
    pair_width = key_self.shape[1]
    hidden = gate_proj.shape[1]
    key_heads = pair_width // HEAD_DIM
    head_count = width // HEAD_DIM
    span = memory.shape[1]
    gain_one, gain_two, gain_three = (g.reshape(1, width) for g in (norm_self, norm_cross, norm_feed))
    memory_rows = memory.reshape(-1, width)
    own_pairs = jnp.concatenate(
        [
            jnp.dot(memory_rows, weight, preferred_element_type=F32).astype(BF16)
            for weight in (key_cross, value_cross)
        ],
        axis=1,
    ).reshape(SLOTS, span, 2 * pair_width)
    other_pairs = lax.ppermute(own_pairs, "mem", [(0, 1), (1, 0)])

    backwards = jnp.roll(distance_bucket[::-1], 1)
    onehot = backwards[None, :] == jnp.arange(BUCKETS)[:, None]
    bias_rows = jnp.sum(jnp.where(onehot[None], bias_table.T[:, :, None], 0.0), axis=1)

    act = ((rows, width), BF16)
    pair = ((rows, pair_width), BF16)
    wide = ((rows, width), F32)
    line = ((1, width), F32)
    broad = ((rows, hidden), BF16)
    h1, q, k, v, att, p, after_self = call(
        self_forward,
        [SMEM] + [VMEM] * 3 + [ANY] * 4,
        [act, act, pair, pair, act, ((key_heads, 2 * rows, rows), F32), wide],
        scratch_like(query_self, key_self, value_self, output_self) + [pltpu.SemaphoreType.DMA((4,))],
    )(is_long, inputs, gain_one, bias_rows, query_self, key_self, value_self, output_self)

    outputs, cross_grad, feed_gain_grad, h2, cq, catt, cp, chosen, h3, activated, gate_grad, up_grad = call(
        cross_and_feed,
        [SMEM] * 2 + [VMEM] * 6 + [ANY] * 5,
        [
            act, wide, line, act, act, act,
            ((key_heads, SLOTS, 2 * SHORT, 2 * span), F32),
            ((SLOTS, 2 * span, 2 * pair_width), BF16),
            act, broad, broad, broad,
        ],
        scratch_like(query_cross, output_cross, gate_proj, up_proj, down_proj)
        + [pltpu.VMEM(*wide), pltpu.VMEM(*wide)]
        + [pltpu.SemaphoreType.DMA((2,)), pltpu.SemaphoreType.DMA((3, hidden // TILE))],
    )(
        is_long, memory_len, after_self, cotangent, own_pairs, other_pairs, gain_two, gain_three,
        query_cross, output_cross, gate_proj, up_proj, down_proj,
    )

    weights = (query_self, key_self, value_self, output_self, query_cross, key_cross, value_cross, output_cross)
    half = ((width, width // 2), BF16)
    half_pair = ((width, pair_width // 2), BF16)
    half_broad = ((width, hidden // 2), BF16)
    full_pair = ((width, pair_width), BF16)
    inputs_grad, memory_grad, diagonals, gain_grads, *grads = call(
        backward,
        [SMEM] + [VMEM] * 22 + [ANY] * 8,
        [
            wide, ((memory_rows.shape[0], width), F32), ((head_count, rows), F32), ((2, width), F32),
            half, half_pair, half_pair, half, half, half, half_broad, half_broad,
            ((hidden, width // 2), BF16), full_pair, full_pair,
        ],
        scratch_like(*weights)
        + [pltpu.VMEM(*act), pltpu.VMEM(*act), pltpu.VMEM(*act), pltpu.VMEM(*pair), pltpu.VMEM(*pair)]
        + [pltpu.VMEM((SLOTS, 2 * span, pair_width), F32)] * 2
        + [pltpu.VMEM(*wide), pltpu.VMEM(*wide), pltpu.SemaphoreType.DMA((8,))],
    )(
        is_long, inputs, after_self, cross_grad, cotangent, gain_one, gain_two,
        h1, q, k, v, att, p, h2, cq, catt, cp, chosen, memory_rows, h3, activated, gate_grad, up_grad,
        *weights,
    )

    small = lax.psum(
        jnp.concatenate(
            [diagonals.reshape(-1, 128), gain_grads.reshape(-1, 128), feed_gain_grad.reshape(-1, 128)]
        ),
        "seq",
    )
    size = width // seq_size
    split = diagonals.size // 128
    gains = lax.dynamic_slice_in_dim(
        small[split:].reshape(3, width), lax.axis_index("seq") * size, size, 1
    )
    bias_table_grad = jnp.einsum(
        "hj,bj->bh", small[:split].reshape(diagonals.shape), onehot.astype(F32), precision=lax.Precision.HIGHEST
    )

    def scattered(grad, axes):
        return lax.psum_scatter(grad.astype(F32), axes, scatter_dimension=0, tiled=True)

    joined = [
        lax.all_gather(scattered(grad, "seq"), "mem", axis=1, tiled=True) for grad in grads[:9]
    ]
    q_g, k_g, v_g, o_g, cq_g, co_g, gate_g, up_g, down_g = joined
    ck_g, cv_g = (scattered(grad, ("seq", "mem")) for grad in grads[9:])
    return (
        outputs,
        inputs_grad,
        memory_grad.reshape(memory.shape),
        gains[0],
        q_g,
        k_g,
        v_g,
        o_g,
        bias_table_grad,
        gains[1],
        cq_g,
        ck_g,
        cv_g,
        co_g,
        gains[2],
        gate_g,
        up_g,
        down_g,
    )


def solution(mesh):
    rows = P("seq", None)
    return jax.shard_map(
        functools.partial(shards, mesh.shape["seq"]),
        mesh=mesh,
        in_specs=(rows, P("seq", "mem", None), rows, P("seq"), P("seq")) + (P(),) * 16,
        out_specs=(rows, rows, P("seq", "mem", None), P("seq"))
        + (rows,) * 4
        + (P(), P("seq"), rows)
        + (P(("seq", "mem"), None),) * 2
        + (rows, P("seq"), rows, rows, rows),
        check_vma=False,
    )
```
